256 devices in a mesh: frame: 32 (over z_hi, x, core), head: 4 (over y), batch: 2 (over z_lo).
Axes of the slice: x: 4, y: 4, z: 8 (z_hi: 4, z_lo: 2; z = z_hi * 2 + z_lo), core: 2. Of those that a mesh axis runs over, the one named last changes fastest.
Arguments:
- new_qkv: bfloat16 [4096, 3, 3072], P(('batch', 'frame', 'head')), parts along dimension 0, may hold values from -16 to 16
- new_pos: int32 [6, 2048], P('batch', 'frame'), parts along dimension 0, may hold values from 0 to 31, as said below
- cache_keys: bfloat16 [2048, 3072], P(('batch', 'frame'), 'head'), parts along dimension 0, may hold values from -48 to 48
- cache_values: bfloat16 [2048, 3072], P(('batch', 'frame'), 'head'), parts along dimension 0, may hold values from -6 to 6
- cache_pos: int32 [6, 1024], P('batch', 'frame'), parts along dimension 0, may hold values from 0 to 31, as said below
- cache_shot: int32 [2048], P(('batch', 'frame')), parts along dimension 0, may hold values from 0 to 2, as said below
- out_weight: bfloat16 [3072, 3072], P('head'), may hold values from -0.4375 to 0.4375
Outputs:
- shot_out: bfloat16 [4096, 3072], P(('batch', 'frame', 'head')), parts along dimension 0
The draws below stay inside these ranges and needn't reach their ends.
There are 2 independent parts, one for each index of `batch`. The reference program is written for one: setup_inputs(seed, part) draws one part's arguments, and reference() takes and returns one part's arrays. A program takes and returns all parts, laid end to end along the dimension named above; an argument that names none is the same for every part. Nothing has to cross between parts.
Inputs may be any that keep to these rules, and one draw needn't show every extreme that they name: `new_pos`: component 0 lies below 8, components 1 and 2 below 32. `cache_pos`: component 0 lies below 8, components 1 and 2 below 32. `cache_shot`: never falls along the cache; every one of the 3 shots is present.
All inputs are finite; a program needn't handle non-finite values.
Results may differ from the reference program's by a relative error of at most 0.015.
The reference program's roundings to bfloat16 on the way count: a program that leaves them out, or rounds other values in their place, can miss the bound.
Values may be sent and summed in bfloat16 or wider, within the bound.
A program may use at most 128 MiB of HBM per device.

```python
import jax
import jax.numpy as jnp
from jax import lax

HEADS = 24
HEAD_DIM = 128
SHOTS = 3
SHOT_FRAMES = 8
GRID = 32
D = 3072
NEW = 2048
CACHE = 1024


def shared_draws(key):
    keys_list = jax.random.split(jax.random.fold_in(key, 11), 8)
    new_pos = jnp.stack([jax.random.randint(keys_list[0], (NEW,), 0, SHOT_FRAMES), jax.random.randint(keys_list[1], (NEW,), 0, GRID), jax.random.randint(keys_list[2], (NEW,), 0, GRID)]).astype(jnp.int32)
    cache_pos = jnp.stack([jax.random.randint(keys_list[3], (CACHE,), 0, SHOT_FRAMES), jax.random.randint(keys_list[4], (CACHE,), 0, GRID), jax.random.randint(keys_list[5], (CACHE,), 0, GRID)]).astype(jnp.int32)
    index = jnp.arange(CACHE, dtype=jnp.int32)
    cache_shot = jnp.zeros((CACHE,), jnp.int32)
    spread = CACHE // (4 * SHOTS)
    for boundary in range(1, SHOTS):
        offset = jax.random.randint(jax.random.fold_in(keys_list[6], boundary), (), -spread, spread + 1)
        cut = boundary * CACHE // SHOTS + offset
        cache_shot = cache_shot + (index >= cut).astype(jnp.int32)
    normal_q = jax.random.normal(keys_list[7], (NEW, D), jnp.float32)
    return (new_pos, cache_pos, cache_shot, normal_q)


def draw_new_pos(key, part):
    return shared_draws(key)[0]


def draw_cache_pos(key, part):
    return shared_draws(key)[1]


def draw_cache_shot(key, part):
    return shared_draws(key)[2]


def draw_new_qkv(key, part):
    new_pos, cache_pos, cache_shot, normal_q = shared_draws(key)
    key = jax.random.fold_in(key, 1)
    first_key, second_key = jax.random.split(key)
    queries = jnp.clip(normal_q * 1.6, -10.0, 10.0)
    keys_new = jnp.clip(jax.random.normal(first_key, (NEW, D), jnp.float32) * 1.6, -10.0, 10.0)
    values_new = jnp.clip(jax.random.normal(second_key, (NEW, D), jnp.float32), -6.0, 6.0)
    return jnp.stack([queries, keys_new, values_new], axis=1).astype(jnp.bfloat16)


def draw_cache_keys(key, part):
    key = jax.random.fold_in(key, 2)
    limit = float(32 + 2048 // HEAD_DIM)
    result = jnp.clip(jax.random.normal(key, (CACHE, D), jnp.float32) * 1.6, -10.0, 10.0)
    return jnp.clip(result, -limit, limit).astype(jnp.bfloat16)


def block_scale(rng, shape, cuts, smallest, top_value):
    factor_of, own = 1.0, jax.random.fold_in(rng, 6)
    for dim, parts in cuts:
        draws = jnp.exp(jax.random.uniform(jax.random.fold_in(own, dim), (parts,), jnp.float32, smallest / len(cuts), top_value / len(cuts)))
        factor_of = factor_of * jnp.repeat(draws, shape[dim] // parts).reshape([-1 if axis == dim else 1 for axis in range(len(shape))])
    return factor_of


def normal_values(key, shape, deviation, bound, cuts=(), held_as=jnp.bfloat16):
    values = deviation * jax.random.normal(key, shape, jnp.float32)
    if cuts:
        values = values * block_scale(key, shape, cuts, -0.22, 0.18)
    return jnp.clip(values, -bound, bound).astype(held_as)


def setup_inputs(seed: int = 0, part: int = 0) -> dict:
    key_list = jax.random.split(jax.random.key(seed), 8)
    part_keys = jax.random.split(jax.random.fold_in(key_list[7], part), 8)
    return {
        "new_qkv": draw_new_qkv(jax.random.fold_in(jax.random.fold_in(key_list[7], part), 71), part),
        "new_pos": draw_new_pos(jax.random.fold_in(jax.random.fold_in(key_list[7], part), 71), part),
        "cache_keys": draw_cache_keys(jax.random.fold_in(jax.random.fold_in(key_list[7], part), 71), part),
        "cache_values": normal_values(part_keys[3], (CACHE, D), 1.0, 6.0, ((0, 32), (1, 4))),
        "cache_pos": draw_cache_pos(jax.random.fold_in(jax.random.fold_in(key_list[7], part), 71), part),
        "cache_shot": draw_cache_shot(jax.random.fold_in(jax.random.fold_in(key_list[7], part), 71), part),
        "out_weight": normal_values(key_list[6], (D, D), (D // 16) ** -0.5, 0.4375, ((0, 4),)),
    }


THETA = 10000.0


def rope_angles(temporal, row_pos, column_pos, feature_width, head_dim):
    lanes = jnp.arange(feature_width, dtype=jnp.int32) % head_dim
    pairs = lanes // 2
    time_pairs = head_dim // 16
    row_pairs = (head_dim // 2 - time_pairs) // 2
    rest_pairs = head_dim // 2 - time_pairs - row_pairs
    in_time = pairs < time_pairs
    in_row = (pairs >= time_pairs) & (pairs < time_pairs + row_pairs)
    pair_float = pairs.astype(jnp.float32)
    exponent = jnp.where(in_time, pair_float / time_pairs,
                         jnp.where(in_row, (pair_float - time_pairs) / row_pairs,
                                   (pair_float - time_pairs - row_pairs) / rest_pairs))
    frequency = jnp.power(jnp.float32(THETA), -exponent)
    position = jnp.where(in_time[None, :], temporal[:, None],
                         jnp.where(in_row[None, :], row_pos[:, None], column_pos[:, None])).astype(jnp.float32)
    return position * frequency[None, :]


def rotate(values_in, angles):
    feature_width = values_in.shape[-1]
    even = (jnp.arange(feature_width, dtype=jnp.int32) % 2) == 0
    partner = jnp.where(even, -jnp.roll(values_in, -1, axis=-1), jnp.roll(values_in, 1, axis=-1))
    return values_in * jnp.cos(angles) + partner * jnp.sin(angles)


def reference(new_qkv, new_pos, cache_keys, cache_values, cache_pos, cache_shot, out_weight):
    new_angles = rope_angles(SHOTS * SHOT_FRAMES + new_pos[0], new_pos[1], new_pos[2], D, HEAD_DIM)
    cache_angles = rope_angles(cache_shot * SHOT_FRAMES + cache_pos[0], cache_pos[1], cache_pos[2], D, HEAD_DIM)
    queries = rotate(new_qkv[:, 0].astype(jnp.float32), new_angles).astype(jnp.bfloat16)
    new_keys = rotate(new_qkv[:, 1].astype(jnp.float32), new_angles).astype(jnp.bfloat16)
    cached_keys = rotate(cache_keys.astype(jnp.float32), cache_angles).astype(jnp.bfloat16)
    keys = jnp.concatenate([cached_keys, new_keys], axis=0)
    values_all = jnp.concatenate([cache_values, new_qkv[:, 2]], axis=0)
    head_queries = jnp.transpose(queries.reshape(NEW, HEADS, HEAD_DIM), (1, 0, 2))
    head_keys = jnp.transpose(keys.reshape(CACHE + NEW, HEADS, HEAD_DIM), (1, 0, 2))
    head_values = jnp.transpose(values_all.reshape(CACHE + NEW, HEADS, HEAD_DIM), (1, 0, 2))
    score_scale = 1.0 / (HEAD_DIM ** 0.5)

    def one_head(operands):
        query_rows, key_rows, value_rows = operands
        scores = jnp.dot(query_rows, key_rows.T, preferred_element_type=jnp.float32) * score_scale
        weights = jnp.exp(scores - jnp.max(scores, axis=1, keepdims=True))
        totals = jnp.sum(weights, axis=1, keepdims=True)
        mixed = jnp.dot(weights.astype(jnp.bfloat16), value_rows, preferred_element_type=jnp.float32)
        return (mixed / totals).astype(jnp.bfloat16)

    attended = lax.map(one_head, (head_queries, head_keys, head_values))
    attended = jnp.transpose(attended, (1, 0, 2)).reshape(NEW, D)
    return jnp.dot(attended, out_weight, preferred_element_type=jnp.float32).astype(jnp.bfloat16)
```

```python
import functools
import math

import jax
import jax.numpy as jnp
from jax import lax
from jax.experimental import pallas as pl
from jax.experimental.pallas import tpu as pltpu
from jax.sharding import PartitionSpec as P

HEAD_DIM = 128
SHOTS = 3
SHOT_FRAMES = 8
THETA = 10000.0
RING = 4
CORES = 2
NEW_ROWS = 16
CACHE_ROWS = 32
HEADS_CORE = 3
CHIP_NEW = RING * CORES * NEW_ROWS
CHIP_CACHE = CORES * CACHE_ROWS
ALL_CACHE = RING * CHIP_CACHE
KEYS = RING * (CHIP_NEW + CHIP_CACHE)
QUERIES = RING * CHIP_NEW
OWN = RING * NEW_ROWS
D = 3072
GROUP = D // RING
CHUNKS = 4
CHUNK = D // CHUNKS
SCALE2 = math.log2(math.e) / math.sqrt(HEAD_DIM)
MESH = pl.DeviceIdType.MESH


def frequencies():
    lanes = lax.broadcasted_iota(jnp.int32, (3, HEAD_DIM), 1)
    part = lax.broadcasted_iota(jnp.int32, (3, HEAD_DIM), 0)
    pairs = lanes // 2
    time_pairs = HEAD_DIM // 16
    row_pairs = (HEAD_DIM // 2 - time_pairs) // 2
    rest_pairs = HEAD_DIM // 2 - time_pairs - row_pairs
    of_part = jnp.where(pairs < time_pairs, 0, jnp.where(pairs < time_pairs + row_pairs, 1, 2))
    pair_float = pairs.astype(jnp.float32)
    exponent = jnp.where(
        of_part == 0,
        pair_float / time_pairs,
        jnp.where(
            of_part == 1,
            (pair_float - time_pairs) / row_pairs,
            (pair_float - time_pairs - row_pairs) / rest_pairs,
        ),
    )
    return jnp.where(of_part == part, jnp.exp(exponent * -math.log(THETA)), 0.0)


def turned(block, cos, sin, even):
    x = block.astype(jnp.float32)
    partner = jnp.where(even, pltpu.roll(x, HEAD_DIM - 1, 1), pltpu.roll(x, 1, 1))
    return (x * cos + partner * sin).astype(jnp.bfloat16)


def kernel(
    qkv_hbm,
    npos_hbm,
    ck_hbm,
    cv_hbm,
    cpos_hbm,
    shot_hbm,
    w_hbm,
    out_ref,
    qkv,
    npos,
    ck,
    cv,
    cpos,
    shot,
    w,
    angles,
    stage,
    cstage,
    kv,
    q,
    o,
    lse,
    lse_t,
    ored,
    lred,
    weights,
    part,
    recv,
    in_sem,
    a_send,
    a_recv,
    c_send,
    c_recv,
    x_send,
    x_recv,
    z_send,
    z_recv,
    o_send,
    o_recv,
    l_send,
    l_recv,
    y_send,
    y_recv,
):
    frame = lax.axis_index("frame")
    y = lax.axis_index("head")
    batch = lax.axis_index("batch")
    core = lax.rem(frame, CORES)
    x = lax.rem(frame // CORES, RING)
    z = frame // (CORES * RING)

    def device(dx, dy, dz, dc):
        to = (lax.rem(z + dz, RING) * RING + lax.rem(x + dx, RING)) * CORES + lax.rem(core + dc, CORES)
        return (to, lax.rem(y + dy, RING), batch)

    barrier = pltpu.get_barrier_semaphore()
    greeted = [(0, 0, 0, 1)]
    for d in (2, 1, 3):
        for dc in (0, 1):
            greeted += [(0, 0, d, dc), (d, 0, 0, dc), (0, d, 0, dc)]
    for g in greeted:
        pl.semaphore_signal(barrier, inc=1, device_id=device(*g), device_id_type=MESH)

    loads = [
        pltpu.make_async_copy(a, b, in_sem.at[i])
        for i, (a, b) in enumerate(
            [(npos_hbm, npos), (cpos_hbm, cpos), (shot_hbm, shot), (qkv_hbm, qkv), (ck_hbm, ck), (cv_hbm, cv), (w_hbm, w)]
        )
    ]
    for load in loads:
        load.start()

    lane = lax.broadcasted_iota(jnp.int32, (1, HEAD_DIM), 1)
    even = lax.rem(lane, 2) == 0
    freq = frequencies()
    for load in loads[:3]:
        load.wait()
    first = lax.broadcasted_iota(jnp.int32, (3, 1), 0) == 0

    def angles_of(pos):
        return lax.dot_general(
            pos.astype(jnp.float32),
            freq,
            (((0,), (0,)), ((), ())),
            precision=lax.Precision.HIGHEST,
            preferred_element_type=jnp.float32,
        )

    angles[0 : RING * NEW_ROWS, :] = angles_of(npos[...] + jnp.where(first, SHOTS * SHOT_FRAMES, 0))
    angle = angles[pl.ds(pl.multiple_of(y * NEW_ROWS, NEW_ROWS), NEW_ROWS), :]
    cos = jnp.cos(angle)
    sin = jnp.where(even, -jnp.sin(angle), jnp.sin(angle))

    for load in loads[3:6]:
        load.wait()

    def rotate_new(i, carry):
        for j in range(HEADS_CORE):
            head = i * HEADS_CORE + j
            lanes = pl.ds(pl.multiple_of(head * HEAD_DIM, HEAD_DIM), HEAD_DIM)
            stage[head, 0] = turned(qkv[0, :, lanes], cos, sin, even)
            stage[head, 1] = turned(qkv[1, :, lanes], cos, sin, even)
            stage[head, 2] = qkv[2, :, lanes]
        return carry

    lax.fori_loop(0, D // (HEAD_DIM * HEADS_CORE), rotate_new, 0)
    pl.semaphore_wait(barrier, len(greeted))

    here = pl.multiple_of(core * OWN + y * NEW_ROWS, NEW_ROWS)
    q_rows = pl.ds(pl.multiple_of(z * CHIP_NEW + here, NEW_ROWS), NEW_ROWS)
    kv_rows = pl.ds(pl.multiple_of(ALL_CACHE + x * CHIP_NEW + here, NEW_ROWS), NEW_ROWS)
    sent = []
    mine = []
    for d in (2, 1, 3, 0):
        for dc in (0, 1):
            k = d * CORES + dc
            heads = pl.ds((lax.rem(y + d, RING) * CORES + lax.rem(core + dc, CORES)) * HEADS_CORE, HEADS_CORE)
            pairs = (
                (stage.at[heads, pl.ds(1, 2)], kv.at[:, :, kv_rows]),
                (stage.at[heads, 0], q.at[:, q_rows]),
            )
            for i, (src, dst) in enumerate(pairs):
                if k:
                    copy = pltpu.make_async_remote_copy(
                        src, dst, a_send.at[i, k], a_recv.at[i, k], device_id=device(0, d, 0, dc), device_id_type=MESH
                    )
                    sent.append(copy)
                else:
                    copy = pltpu.make_async_copy(src, dst, a_recv.at[i, k])
                    mine.append(copy)
                copy.start()
    arriving = list(sent)

    angle = angles_of(cpos[...] + jnp.where(first, shot[...] * SHOT_FRAMES, 0))
    cos = jnp.cos(angle)
    sin = jnp.where(even, -jnp.sin(angle), jnp.sin(angle))
    for head in range(GROUP // HEAD_DIM):
        lanes = slice(head * HEAD_DIM, (head + 1) * HEAD_DIM)
        cstage[head, 0] = turned(ck[:, lanes], cos, sin, even)
        cstage[head, 1] = cv[:, lanes]
    c_rows = pl.ds(pl.multiple_of(x * CHIP_CACHE + core * CACHE_ROWS, CACHE_ROWS), CACHE_ROWS)
    cached = []
    for d in (2, 1, 3, 0):
        for dc in (0, 1):
            k = d * CORES + dc
            src = cstage.at[pl.ds(lax.rem(core + dc, CORES) * HEADS_CORE, HEADS_CORE)]
            dst = kv.at[:, :, c_rows]
            if k:
                copy = pltpu.make_async_remote_copy(
                    src, dst, c_send.at[k], c_recv.at[k], device_id=device(d, 0, 0, dc), device_id_type=MESH
                )
                cached.append(copy)
            else:
                copy = pltpu.make_async_copy(src, dst, c_recv.at[k])
                mine.append(copy)
            copy.start()
    sent += cached

    for copy in mine:
        copy.wait()
    for copy in arriving:
        copy.wait_recv()

    chip_kv = pl.ds(pl.multiple_of(ALL_CACHE + x * CHIP_NEW, CHIP_NEW), CHIP_NEW)
    chip_q = pl.ds(pl.multiple_of(z * CHIP_NEW, CHIP_NEW), CHIP_NEW)
    gathered = []
    for head in range(HEADS_CORE):
        of_head = []
        for d in (2, 1, 3):
            of_head.append(
                pltpu.make_async_remote_copy(
                    q.at[head, chip_q],
                    q.at[head, chip_q],
                    z_send.at[head, d],
                    z_recv.at[head, d],
                    device_id=device(0, 0, d, 0),
                    device_id_type=MESH,
                )
            )
            of_head.append(
                pltpu.make_async_remote_copy(
                    kv.at[head, :, chip_kv],
                    kv.at[head, :, chip_kv],
                    x_send.at[head, d],
                    x_recv.at[head, d],
                    device_id=device(d, 0, 0, 0),
                    device_id_type=MESH,
                )
            )
        for copy in of_head:
            copy.start()
        gathered.append(of_head)
        sent += of_head
    for copy in cached:
        copy.wait_recv()

    def o_copy(head, d, dc):
        to_z = lax.rem(z + d, RING)
        to_core = lax.rem(core + dc, CORES)
        rows = pl.ds(pl.multiple_of(to_z * CHIP_NEW + to_core * OWN, OWN), OWN)
        k = d * CORES + dc
        return pltpu.make_async_remote_copy(
            o.at[head, rows],
            ored.at[z, core, head],
            o_send.at[head, k],
            o_recv.at[head, k],
            device_id=device(0, 0, d, dc),
            device_id_type=MESH,
        )

    for head in range(HEADS_CORE):
        for copy in gathered[head]:
            copy.wait_recv()

        def attend(t, carry, head=head):
            d = lax.rem(RING + 2 - t, RING)
            to_z = lax.rem(z + d, RING)
            rows = pl.ds(pl.multiple_of(to_z * CHIP_NEW, CHIP_NEW), CHIP_NEW)
            scores = lax.dot_general(
                q[head, rows], kv[head, 0], (((1,), (1,)), ((), ())), preferred_element_type=jnp.float32
            )
            peak = jnp.max(scores, axis=1, keepdims=True)
            p = jnp.exp2((scores - peak) * SCALE2)
            total = jnp.sum(p, axis=1, keepdims=True)
            mixed = jnp.dot(p.astype(jnp.bfloat16), kv[head, 1], preferred_element_type=jnp.float32)
            o[head, rows] = (mixed / total).astype(jnp.bfloat16)
            level = peak * SCALE2 + jnp.log2(total)
            lse[rows, :] = jnp.where(lane == head, level, lse[rows, :] if head else 0.0)
            own = pl.ds(pl.multiple_of(to_z * CHIP_NEW + core * OWN, OWN), OWN)

            o_copy(head, d, 1).start()

            @pl.when(d != 0)
            def _():
                o_copy(head, d, 0).start()

            @pl.when(d == 0)
            def _():
                ored[z, core, head] = o[head, own]

            return carry

        lax.fori_loop(0, RING, attend, 0)

    stats = []
    for d in (2, 1, 3, 0):
        to_z = lax.rem(z + d, RING)
        rows = pl.ds(pl.multiple_of(to_z * CHIP_NEW, CHIP_NEW), CHIP_NEW)
        lse_t[to_z] = jnp.transpose(lse[rows, :])[0:8, :]
        for dc in (0, 1):
            k = d * CORES + dc
            if k:
                copy = pltpu.make_async_remote_copy(
                    lse_t.at[to_z],
                    lred.at[z, core],
                    l_send.at[k],
                    l_recv.at[k],
                    device_id=device(0, 0, d, dc),
                    device_id_type=MESH,
                )
                copy.start()
                stats.append(copy)
    lred[z, core] = lse_t[z]
    sent += stats

    for copy in stats:
        copy.wait_recv()
    levels = lred[...]
    share = jnp.exp2(levels - jnp.max(levels, axis=0, keepdims=True))
    share = share / jnp.sum(share, axis=0, keepdims=True)
    columns = jnp.transpose(share.reshape(RING * CORES * 8, CHIP_NEW))
    weights[:, 0 : RING * CORES * 8] = columns
    mine_w = weights[pl.ds(pl.multiple_of(core * OWN, OWN), OWN), :]
    returned = [o_copy(head, d, dc) for head in range(HEADS_CORE) for d in (2, 1, 3, 0) for dc in (0, 1) if d or dc]
    for copy in returned:
        copy.wait_recv()
    sent += returned
    attended = []
    for c in range(CORES):
        for head in range(HEADS_CORE):
            total = None
            for s in range(RING):
                at = (s * CORES + c) * 8 + head
                term = ored[s, c, head].astype(jnp.float32) * mine_w[:, at : at + 1]
                total = term if total is None else total + term
            attended.append(total.astype(jnp.bfloat16))
    attended = jnp.concatenate(attended, axis=1)

    loads[6].wait()
    summed = []
    for j in range(CHUNKS):
        cols = slice(j * CHUNK, (j + 1) * CHUNK)
        part[:, cols] = jnp.dot(attended, w[:, cols], preferred_element_type=jnp.float32).astype(jnp.bfloat16)
        of_chunk = []
        for d in (2, 1, 3):
            rows = pl.ds(pl.multiple_of(lax.rem(y + d, RING) * NEW_ROWS, NEW_ROWS), NEW_ROWS)
            copy = pltpu.make_async_remote_copy(
                part.at[rows, pl.ds(j * CHUNK, CHUNK)],
                recv.at[d, :, pl.ds(j * CHUNK, CHUNK)],
                y_send.at[j, d],
                y_recv.at[j, d],
                device_id=device(0, d, 0, 0),
                device_id_type=MESH,
            )
            copy.start()
            of_chunk.append(copy)
        summed.append(of_chunk)
        sent += of_chunk
    rows = pl.ds(pl.multiple_of(y * NEW_ROWS, NEW_ROWS), NEW_ROWS)
    for j in range(CHUNKS):
        cols = slice(j * CHUNK, (j + 1) * CHUNK)
        for copy in summed[j]:
            copy.wait_recv()
        total = part[rows, cols].astype(jnp.float32)
        for d in (1, 2, 3):
            total = total + recv[d, :, cols].astype(jnp.float32)
        out_ref[:, cols] = total.astype(jnp.bfloat16)

    for copy in sent:
        copy.wait_send()


def on_device(new_qkv, new_pos, cache_keys, cache_values, cache_pos, cache_shot, out_weight):
    bf16, f32, i32 = jnp.bfloat16, jnp.float32, jnp.int32
    dma = pltpu.SemaphoreType.DMA
    partners = RING * CORES
    return pl.pallas_call(
        kernel,
        out_shape=jax.ShapeDtypeStruct((NEW_ROWS, D), bf16),
        in_specs=[pl.BlockSpec(memory_space=pl.ANY)] * 7,
        out_specs=pl.BlockSpec(memory_space=pltpu.VMEM),
        scratch_shapes=[
            pltpu.VMEM((3, NEW_ROWS, D), bf16),
            pltpu.VMEM((3, RING * NEW_ROWS), i32),
            pltpu.VMEM((CACHE_ROWS, GROUP), bf16),
            pltpu.VMEM((CACHE_ROWS, GROUP), bf16),
            pltpu.VMEM((3, CACHE_ROWS), i32),
            pltpu.VMEM((1, CACHE_ROWS), i32),
            pltpu.VMEM((GROUP, D), bf16),
            pltpu.VMEM((RING * NEW_ROWS, HEAD_DIM), f32),
            pltpu.VMEM((D // HEAD_DIM, 3, NEW_ROWS, HEAD_DIM), bf16),
            pltpu.VMEM((GROUP // HEAD_DIM, 2, CACHE_ROWS, HEAD_DIM), bf16),
            pltpu.VMEM((HEADS_CORE, 2, KEYS, HEAD_DIM), bf16),
            pltpu.VMEM((HEADS_CORE, QUERIES, HEAD_DIM), bf16),
            pltpu.VMEM((HEADS_CORE, QUERIES, HEAD_DIM), bf16),
            pltpu.VMEM((QUERIES, HEAD_DIM), f32),
            pltpu.VMEM((RING, 8, CHIP_NEW), f32),
            pltpu.VMEM((RING, CORES, HEADS_CORE, OWN, HEAD_DIM), bf16),
            pltpu.VMEM((RING, CORES, 8, CHIP_NEW), f32),
            pltpu.VMEM((CHIP_NEW, HEAD_DIM), f32),
            pltpu.VMEM((OWN, D), bf16),
            pltpu.VMEM((RING, NEW_ROWS, D), bf16),
            dma((7,)),
            dma((2, partners)),
            dma((2, partners)),
            dma((partners,)),
            dma((partners,)),
            dma((HEADS_CORE, RING)),
            dma((HEADS_CORE, RING)),
            dma((HEADS_CORE, RING)),
            dma((HEADS_CORE, RING)),
            dma((HEADS_CORE, partners)),
            dma((HEADS_CORE, partners)),
            dma((partners,)),
            dma((partners,)),
            dma((CHUNKS, RING)),
            dma((CHUNKS, RING)),
        ],
        compiler_params=pltpu.CompilerParams(collective_id=0, has_side_effects=True, vmem_limit_bytes=63 << 20),
        name="shot_attention",
    )(
        jnp.transpose(new_qkv, (1, 0, 2)),
        new_pos,
        cache_keys,
        cache_values,
        cache_pos,
        cache_shot.reshape(1, CACHE_ROWS),
        out_weight,
    )


def solution(mesh):
    placed = (
        P(("batch", "frame", "head"), None, None),
        P("batch", "frame"),
        P(("batch", "frame"), "head"),
        P(("batch", "frame"), "head"),
        P("batch", "frame"),
        P(("batch", "frame")),
        P("head", None),
    )
    return jax.shard_map(
        on_device,
        mesh=mesh,
        in_specs=placed,
        out_specs=P(("batch", "frame", "head"), None),
        check_vma=False,
    )
```

```python
import functools
import math

import jax
import jax.numpy as jnp
from jax import lax
from jax.experimental import pallas as pl
from jax.experimental.pallas import tpu as pltpu
from jax.sharding import PartitionSpec as P

HEAD_DIM = 128
SHOTS = 3
SHOT_FRAMES = 8
THETA = 10000.0
RING = 4
CORES = 2
NEW_ROWS = 16
CACHE_ROWS = 32
HEADS_CORE = 3
CHIP_NEW = RING * CORES * NEW_ROWS
CHIP_CACHE = CORES * CACHE_ROWS
ALL_CACHE = RING * CHIP_CACHE
KEYS = RING * (CHIP_NEW + CHIP_CACHE)
QUERIES = RING * CHIP_NEW
OWN = RING * NEW_ROWS
D = 3072
GROUP = D // RING
CHUNKS = 4
CHUNK = D // CHUNKS
SCALE2 = math.log2(math.e) / math.sqrt(HEAD_DIM)
MESH = pl.DeviceIdType.MESH


def frequencies():
    lanes = lax.broadcasted_iota(jnp.int32, (3, HEAD_DIM), 1)
    part = lax.broadcasted_iota(jnp.int32, (3, HEAD_DIM), 0)
    pairs = lanes // 2
    time_pairs = HEAD_DIM // 16
    row_pairs = (HEAD_DIM // 2 - time_pairs) // 2
    rest_pairs = HEAD_DIM // 2 - time_pairs - row_pairs
    of_part = jnp.where(pairs < time_pairs, 0, jnp.where(pairs < time_pairs + row_pairs, 1, 2))
    pair_float = pairs.astype(jnp.float32)
    exponent = jnp.where(
        of_part == 0,
        pair_float / time_pairs,
        jnp.where(
            of_part == 1,
            (pair_float - time_pairs) / row_pairs,
            (pair_float - time_pairs - row_pairs) / rest_pairs,
        ),
    )
    return jnp.where(of_part == part, jnp.exp(exponent * -math.log(THETA)), 0.0)


def turned(block, cos, sin, even):
    x = block.astype(jnp.float32)
    partner = jnp.where(even, pltpu.roll(x, HEAD_DIM - 1, 1), pltpu.roll(x, 1, 1))
    return (x * cos + partner * sin).astype(jnp.bfloat16)


def kernel(
    qkv_hbm,
    npos_hbm,
    ck_hbm,
    cv_hbm,
    cpos_hbm,
    shot_hbm,
    w_hbm,
    out_ref,
    qkv,
    npos,
    ck,
    cv,
    cpos,
    shot,
    w,
    angles,
    stage,
    cstage,
    kv,
    q,
    o,
    lse,
    lse_t,
    ored,
    lred,
    weights,
    part,
    recv,
    in_sem,
    heard,
    f_send,
    f_recv,
    a_send,
    a_recv,
    c_send,
    c_recv,
    x_send,
    x_recv,
    z_send,
    z_recv,
    o_send,
    o_recv,
    l_send,
    l_recv,
    y_send,
    y_recv,
):
    frame = lax.axis_index("frame")
    y = lax.axis_index("head")
    batch = lax.axis_index("batch")
    core = lax.rem(frame, CORES)
    x = lax.rem(frame // CORES, RING)
    z = frame // (CORES * RING)

    def device(dx, dy, dz, dc):
        to = (lax.rem(z + dz, RING) * RING + lax.rem(x + dx, RING)) * CORES + lax.rem(core + dc, CORES)
        return (to, lax.rem(y + dy, RING), batch)

    def partners():
        for to_core in (0, 1):
            for d in (2, 1, 3):
                yield d, lax.rem(core + to_core, CORES)
        yield 0, 1

    barrier = pltpu.get_barrier_semaphore()
    crossed = [(0, dy, dz, c) for dz in (2, 1, 3, 0) for c in (0, 1) for dy in (2, 1, 3, 0) if dy or dz or c]
    greeted = [(0, 0, 0, 1)]
    for d in (2, 1, 3):
        for dc in (0, 1):
            greeted += [(0, 0, d, dc), (d, 0, 0, dc), (0, d, 0, dc)]
    for g in greeted:
        pl.semaphore_signal(barrier, inc=1, device_id=device(*g), device_id_type=MESH)

    loads = [
        pltpu.make_async_copy(a, b, in_sem.at[i])
        for i, (a, b) in enumerate(
            [(npos_hbm, npos), (cpos_hbm, cpos), (shot_hbm, shot), (qkv_hbm, qkv), (ck_hbm, ck), (cv_hbm, cv), (w_hbm, w)]
        )
    ]
    for load in loads:
        load.start()

    lane = lax.broadcasted_iota(jnp.int32, (1, HEAD_DIM), 1)
    even = lax.rem(lane, 2) == 0
    freq = frequencies()
    for load in loads[:3]:
        load.wait()
    first = lax.broadcasted_iota(jnp.int32, (3, 1), 0) == 0

    def angles_of(pos):
        return lax.dot_general(
            pos.astype(jnp.float32),
            freq,
            (((0,), (0,)), ((), ())),
            precision=lax.Precision.HIGHEST,
            preferred_element_type=jnp.float32,
        )

    angles[0 : RING * NEW_ROWS, :] = angles_of(npos[...] + jnp.where(first, SHOTS * SHOT_FRAMES, 0))
    angle = angles[pl.ds(pl.multiple_of(y * NEW_ROWS, NEW_ROWS), NEW_ROWS), :]
    cos = jnp.cos(angle)
    sin = jnp.where(even, -jnp.sin(angle), jnp.sin(angle))

    for load in loads[3:6]:
        load.wait()

    def rotate_new(i, carry):
        for j in range(HEADS_CORE):
            head = i * HEADS_CORE + j
            lanes = pl.ds(pl.multiple_of(head * HEAD_DIM, HEAD_DIM), HEAD_DIM)
            stage[head, 0] = turned(qkv[0, :, lanes], cos, sin, even)
            stage[head, 1] = turned(qkv[1, :, lanes], cos, sin, even)
            stage[head, 2] = qkv[2, :, lanes]
        return carry

    lax.fori_loop(0, D // (HEAD_DIM * HEADS_CORE), rotate_new, 0)
    angle = angles_of(cpos[...] + jnp.where(first, shot[...] * SHOT_FRAMES, 0))
    cos = jnp.cos(angle)
    sin = jnp.where(even, -jnp.sin(angle), jnp.sin(angle))
    for head in range(GROUP // HEAD_DIM):
        lanes = slice(head * HEAD_DIM, (head + 1) * HEAD_DIM)
        cstage[head, 0] = turned(ck[:, lanes], cos, sin, even)
        cstage[head, 1] = cv[:, lanes]
    pl.semaphore_wait(barrier, len(greeted))
    for d in (2, 1, 3):
        pl.semaphore_signal(heard, inc=1, device_id=device(0, d, 0, 0), device_id_type=MESH)

    here = pl.multiple_of(core * OWN + y * NEW_ROWS, NEW_ROWS)
    q_rows = pl.ds(pl.multiple_of(z * CHIP_NEW + here, NEW_ROWS), NEW_ROWS)
    kv_rows = pl.ds(pl.multiple_of(ALL_CACHE + x * CHIP_NEW + here, NEW_ROWS), NEW_ROWS)
    sent = []

    def scatter(sems, offsets, parts):
        copies = []
        for d, dc in partners():
            k = d * CORES + dc
            src, dst, to = parts(d, dc)
            copy = pltpu.make_async_remote_copy(
                src, dst, sems[0].at[offsets, k], sems[1].at[offsets, k], device_id=to, device_id_type=MESH
            )
            sent.append(copy)
            copy.start()
            copies.append(copy)
        src, dst, _ = parts(0, 0)
        copy = pltpu.make_async_copy(src, dst, sems[1].at[offsets, 0])
        copy.start()
        copies.append(copy)
        return copies

    def arrive(copies):
        for copy in copies[:-1]:
            copy.wait_recv()
        copies[-1].wait()

    def new_part(first, heads, of_q):
        def parts(d, dc):
            to = (lax.rem(y + d, RING) * CORES + lax.rem(core + dc, CORES)) * HEADS_CORE
            src = stage.at[pl.ds(to + first, heads)]
            own = pl.ds(first, heads)
            if of_q:
                return src.at[:, 0], q.at[own, q_rows], device(0, d, 0, dc)
            return src.at[:, pl.ds(1, 2)], kv.at[own, :, kv_rows], device(0, d, 0, dc)

        return parts

    def cache_part(d, dc):
        src = cstage.at[pl.ds(lax.rem(core + dc, CORES) * HEADS_CORE, HEADS_CORE)]
        return src, kv.at[:, :, c_rows], device(d, 0, 0, dc)

    c_rows = pl.ds(pl.multiple_of(x * CHIP_CACHE + core * CACHE_ROWS, CACHE_ROWS), CACHE_ROWS)
    chip_kv = pl.ds(pl.multiple_of(ALL_CACHE + x * CHIP_NEW, CHIP_NEW), CHIP_NEW)
    chip_q = pl.ds(pl.multiple_of(z * CHIP_NEW, CHIP_NEW), CHIP_NEW)

    def along_x(head):
        copies = [
            pltpu.make_async_remote_copy(
                kv.at[head, :, chip_kv],
                kv.at[head, :, chip_kv],
                x_send.at[head, d],
                x_recv.at[head, d],
                device_id=device(d, 0, 0, 0),
                device_id_type=MESH,
            )
            for d in (2, 1, 3)
        ]
        for copy in copies:
            copy.start()
        sent.extend(copies)
        return copies

    def along_z(head):
        copies = [
            pltpu.make_async_remote_copy(
                q.at[head, chip_q],
                q.at[head, chip_q],
                z_send.at[head, d],
                z_recv.at[head, d],
                device_id=device(0, 0, d, 0),
                device_id_type=MESH,
            )
            for d in (2, 1, 3)
        ]
        for copy in copies:
            copy.start()
        sent.extend(copies)
        return copies

    a_sems = (a_send, a_recv)
    kv_in = [scatter(a_sems, 1, new_part(0, 1, False))]
    cached = scatter((c_send, c_recv), 0, cache_part)
    q_in = scatter(a_sems, 0, new_part(1, 2, True))
    kv_in.append(scatter(a_sems, 2, new_part(1, 2, False)))
    pl.semaphore_wait(heard, 3)
    straight = []
    for dx, dy, dz, at_core in crossed:
        dc = lax.rem(core + at_core, CORES) if dy or dz else 1
        to = (lax.rem(y + dy, RING) * CORES + lax.rem(core + dc, CORES)) * HEADS_CORE
        copy = pltpu.make_async_remote_copy(
            stage.at[to, 0],
            q.at[0, q_rows],
            f_send.at[0],
            f_recv.at[0],
            device_id=device(dx, dy, dz, dc),
            device_id_type=MESH,
        )
        copy.start()
    own_q = pltpu.make_async_copy(stage.at[(y * CORES + core) * HEADS_CORE, 0], q.at[0, q_rows], f_recv.at[1])
    own_q.start()

    arrive(kv_in[0])
    gathered_x = [along_x(0)]
    arrive(q_in)
    gathered_z = [[], along_z(1), along_z(2)]
    arrive(kv_in[1])
    gathered_x += [along_x(1), along_x(2)]
    arrive(cached)
    whole = q.at[0, pl.ds(0, QUERIES - NEW_ROWS)]
    pltpu.make_async_copy(whole, whole, f_recv.at[0]).wait()
    own_q.wait()

    def o_copy(head, d, dc):
        to_z = lax.rem(z + d, RING)
        to_core = lax.rem(core + dc, CORES)
        rows = pl.ds(pl.multiple_of(to_z * CHIP_NEW + to_core * OWN, OWN), OWN)
        k = d * CORES + dc
        return pltpu.make_async_remote_copy(
            o.at[head, rows],
            ored.at[z, core, head],
            o_send.at[head, k],
            o_recv.at[head, k],
            device_id=device(0, 0, d, dc),
            device_id_type=MESH,
        )

    for head in range(HEADS_CORE):
        for copy in gathered_x[head] + gathered_z[head]:
            copy.wait_recv()
        scores = lax.dot_general(q[head], kv[head, 0], (((1,), (1,)), ((), ())), preferred_element_type=jnp.float32)
        peak = jnp.max(scores, axis=1, keepdims=True)
        p = jnp.exp2((scores - peak) * SCALE2)
        total = jnp.sum(p, axis=1, keepdims=True)
        level = peak * SCALE2 + jnp.log2(total)
        lse[...] = jnp.where(lane == head, level, lse[...] if head else 0.0)
        if head == HEADS_CORE - 1:
            stats = []
            for s in range(RING):
                lse_t[s] = jnp.transpose(lse[s * CHIP_NEW : (s + 1) * CHIP_NEW, :])[0:8, :]
            for d, dc in partners():
                k = d * CORES + dc
                copy = pltpu.make_async_remote_copy(
                    lse_t.at[lax.rem(z + d, RING)],
                    lred.at[z, core],
                    l_send.at[k],
                    l_recv.at[k],
                    device_id=device(0, 0, d, dc),
                    device_id_type=MESH,
                )
                copy.start()
                stats.append(copy)
            lred[z, core] = lse_t[z]
            sent += stats
        mixed = jnp.dot(p.astype(jnp.bfloat16), kv[head, 1], preferred_element_type=jnp.float32)
        o[head] = (mixed / total).astype(jnp.bfloat16)
        for d, dc in partners():
            o_copy(head, d, dc).start()
        own = pl.ds(pl.multiple_of(z * CHIP_NEW + core * OWN, OWN), OWN)
        ored[z, core, head] = o[head, own]

    for copy in stats:
        copy.wait_recv()
    levels = lred[...]
    share = jnp.exp2(levels - jnp.max(levels, axis=0, keepdims=True))
    share = share / jnp.sum(share, axis=0, keepdims=True)
    columns = jnp.transpose(share.reshape(RING * CORES * 8, CHIP_NEW))
    weights[:, 0 : RING * CORES * 8] = columns
    mine_w = weights[pl.ds(pl.multiple_of(core * OWN, OWN), OWN), :]
    returned = [o_copy(head, d, dc) for head in range(HEADS_CORE) for d, dc in partners()]
    for copy in returned:
        copy.wait_recv()
    sent += returned
    attended = []
    for c in range(CORES):
        for head in range(HEADS_CORE):
            total = None
            for s in range(RING):
                at = (s * CORES + c) * 8 + head
                term = ored[s, c, head].astype(jnp.float32) * mine_w[:, at : at + 1]
                total = term if total is None else total + term
            attended.append(total.astype(jnp.bfloat16))
    attended = jnp.concatenate(attended, axis=1)

    loads[6].wait()
    summed = []
    for j in range(CHUNKS):
        cols = slice(j * CHUNK, (j + 1) * CHUNK)
        part[:, cols] = jnp.dot(attended, w[:, cols], preferred_element_type=jnp.float32).astype(jnp.bfloat16)
        of_chunk = []
        for d in (2, 1, 3):
            rows = pl.ds(pl.multiple_of(lax.rem(y + d, RING) * NEW_ROWS, NEW_ROWS), NEW_ROWS)
            copy = pltpu.make_async_remote_copy(
                part.at[rows, pl.ds(j * CHUNK, CHUNK)],
                recv.at[d, :, pl.ds(j * CHUNK, CHUNK)],
                y_send.at[j, d],
                y_recv.at[j, d],
                device_id=device(0, d, 0, 0),
                device_id_type=MESH,
            )
            copy.start()
            of_chunk.append(copy)
        summed.append(of_chunk)
        sent += of_chunk
    rows = pl.ds(pl.multiple_of(y * NEW_ROWS, NEW_ROWS), NEW_ROWS)
    for j in range(CHUNKS):
        cols = slice(j * CHUNK, (j + 1) * CHUNK)
        for copy in summed[j]:
            copy.wait_recv()
        total = part[rows, cols].astype(jnp.float32)
        for d in (1, 2, 3):
            total = total + recv[d, :, cols].astype(jnp.float32)
        out_ref[:, cols] = total.astype(jnp.bfloat16)

    for copy in sent:
        copy.wait_send()
    pltpu.make_async_copy(whole, whole, f_send.at[0]).wait()


def on_device(new_qkv, new_pos, cache_keys, cache_values, cache_pos, cache_shot, out_weight):
    bf16, f32, i32 = jnp.bfloat16, jnp.float32, jnp.int32
    dma = pltpu.SemaphoreType.DMA
    partners = RING * CORES
    return pl.pallas_call(
        kernel,
        out_shape=jax.ShapeDtypeStruct((NEW_ROWS, D), bf16),
        in_specs=[pl.BlockSpec(memory_space=pl.ANY)] * 7,
        out_specs=pl.BlockSpec(memory_space=pltpu.VMEM),
        scratch_shapes=[
            pltpu.VMEM((3, NEW_ROWS, D), bf16),
            pltpu.VMEM((3, RING * NEW_ROWS), i32),
            pltpu.VMEM((CACHE_ROWS, GROUP), bf16),
            pltpu.VMEM((CACHE_ROWS, GROUP), bf16),
            pltpu.VMEM((3, CACHE_ROWS), i32),
            pltpu.VMEM((1, CACHE_ROWS), i32),
            pltpu.VMEM((GROUP, D), bf16),
            pltpu.VMEM((RING * NEW_ROWS, HEAD_DIM), f32),
            pltpu.VMEM((D // HEAD_DIM, 3, NEW_ROWS, HEAD_DIM), bf16),
            pltpu.VMEM((GROUP // HEAD_DIM, 2, CACHE_ROWS, HEAD_DIM), bf16),
            pltpu.VMEM((HEADS_CORE, 2, KEYS, HEAD_DIM), bf16),
            pltpu.VMEM((HEADS_CORE, QUERIES, HEAD_DIM), bf16),
            pltpu.VMEM((HEADS_CORE, QUERIES, HEAD_DIM), bf16),
            pltpu.VMEM((QUERIES, HEAD_DIM), f32),
            pltpu.VMEM((RING, 8, CHIP_NEW), f32),
            pltpu.VMEM((RING, CORES, HEADS_CORE, OWN, HEAD_DIM), bf16),
            pltpu.VMEM((RING, CORES, 8, CHIP_NEW), f32),
            pltpu.VMEM((CHIP_NEW, HEAD_DIM), f32),
            pltpu.VMEM((OWN, D), bf16),
            pltpu.VMEM((RING, NEW_ROWS, D), bf16),
            dma((7,)),
            pltpu.SemaphoreType.REGULAR,
            dma((1,)),
            dma((2,)),
            dma((4, partners)),
            dma((4, partners)),
            dma((1, partners)),
            dma((1, partners)),
            dma((HEADS_CORE, RING)),
            dma((HEADS_CORE, RING)),
            dma((HEADS_CORE, RING)),
            dma((HEADS_CORE, RING)),
            dma((HEADS_CORE, partners)),
            dma((HEADS_CORE, partners)),
            dma((partners,)),
            dma((partners,)),
            dma((CHUNKS, RING)),
            dma((CHUNKS, RING)),
        ],
        compiler_params=pltpu.CompilerParams(collective_id=0, has_side_effects=True, vmem_limit_bytes=32 << 20),
        name="shot_attention",
    )(
        *(
            pltpu.with_memory_space_constraint(a, pltpu.HBM)
            for a in (
                jnp.transpose(new_qkv, (1, 0, 2)),
                new_pos,
                cache_keys,
                cache_values,
                cache_pos,
                cache_shot.reshape(1, CACHE_ROWS),
                out_weight,
            )
        )
    )


def solution(mesh):
    placed = (
        P(("batch", "frame", "head"), None, None),
        P("batch", "frame"),
        P(("batch", "frame"), "head"),
        P(("batch", "frame"), "head"),
        P("batch", "frame"),
        P(("batch", "frame")),
        P("head", None),
    )
    return jax.shard_map(
        on_device,
        mesh=mesh,
        in_specs=placed,
        out_specs=P(("batch", "frame", "head"), None),
        check_vma=False,
    )
```

```python
import functools
import math

import jax
import jax.numpy as jnp
from jax import lax
from jax.experimental import pallas as pl
from jax.experimental.pallas import tpu as pltpu
from jax.sharding import PartitionSpec as P

HEAD_DIM = 128
SHOTS = 3
SHOT_FRAMES = 8
THETA = 10000.0
RING = 4
CORES = 2
NEW_ROWS = 16
CACHE_ROWS = 32
HEADS_CORE = 3
CHIP_NEW = RING * CORES * NEW_ROWS
CHIP_CACHE = CORES * CACHE_ROWS
ALL_CACHE = RING * CHIP_CACHE
KEYS = RING * (CHIP_NEW + CHIP_CACHE)
QUERIES = RING * CHIP_NEW
OWN = RING * NEW_ROWS
D = 3072
GROUP = D // RING
CHUNKS = 4
CHUNK = D // CHUNKS
SCALE2 = math.log2(math.e) / math.sqrt(HEAD_DIM)
MESH = pl.DeviceIdType.MESH


def frequencies():
    lanes = lax.broadcasted_iota(jnp.int32, (3, HEAD_DIM), 1)
    part = lax.broadcasted_iota(jnp.int32, (3, HEAD_DIM), 0)
    pairs = lanes // 2
    time_pairs = HEAD_DIM // 16
    row_pairs = (HEAD_DIM // 2 - time_pairs) // 2
    rest_pairs = HEAD_DIM // 2 - time_pairs - row_pairs
    of_part = jnp.where(pairs < time_pairs, 0, jnp.where(pairs < time_pairs + row_pairs, 1, 2))
    pair_float = pairs.astype(jnp.float32)
    exponent = jnp.where(
        of_part == 0,
        pair_float / time_pairs,
        jnp.where(
            of_part == 1,
            (pair_float - time_pairs) / row_pairs,
            (pair_float - time_pairs - row_pairs) / rest_pairs,
        ),
    )
    return jnp.where(of_part == part, jnp.exp(exponent * -math.log(THETA)), 0.0)


def turned(block, cos, sin, even):
    x = block.astype(jnp.float32)
    partner = jnp.where(even, pltpu.roll(x, HEAD_DIM - 1, 1), pltpu.roll(x, 1, 1))
    return (x * cos + partner * sin).astype(jnp.bfloat16)


def kernel(
    qkv_hbm,
    npos_hbm,
    ck_hbm,
    cv_hbm,
    cpos_hbm,
    shot_hbm,
    w_hbm,
    out_ref,
    qkv,
    npos,
    ck,
    cv,
    cpos,
    shot,
    w,
    angles,
    stage,
    cstage,
    kv,
    q,
    o,
    lse,
    lse_t,
    ored,
    lred,
    weights,
    part,
    recv,
    in_sem,
    heard,
    told,
    f_send,
    f_recv,
    a_send,
    a_recv,
    c_send,
    c_recv,
    x_send,
    x_recv,
    z_send,
    z_recv,
    o_send,
    o_recv,
    l_send,
    l_recv,
    y_send,
    y_recv,
):
    frame = lax.axis_index("frame")
    y = lax.axis_index("head")
    batch = lax.axis_index("batch")
    core = lax.rem(frame, CORES)
    x = lax.rem(frame // CORES, RING)
    z = frame // (CORES * RING)

    def device(dx, dy, dz, dc):
        to = (lax.rem(z + dz, RING) * RING + lax.rem(x + dx, RING)) * CORES + lax.rem(core + dc, CORES)
        return (to, lax.rem(y + dy, RING), batch)

    def partners():
        for to_core in (0, 1):
            for d in (2, 1, 3):
                yield d, lax.rem(core + to_core, CORES)
        yield 0, 1

    barrier = pltpu.get_barrier_semaphore()
    for d in (2, 1, 3):
        pl.semaphore_signal(barrier, inc=1, device_id=device(0, 0, d, core), device_id_type=MESH)
    for d in (2, 1, 3):
        pl.semaphore_signal(barrier, inc=1, device_id=device(0, d, 0, 1 - core), device_id_type=MESH)
        pl.semaphore_signal(barrier, inc=1, device_id=device(d, 0, 0, 1 - core), device_id_type=MESH)
    pl.semaphore_signal(barrier, inc=1, device_id=device(0, 0, 0, 1), device_id_type=MESH)

    crossed = [(0, dy, dz, c) for dz in (2, 1, 3, 0) for c in (0, 1) for dy in (2, 1, 3, 0) if dy or dz or c]
    loads = [
        pltpu.make_async_copy(a, b, in_sem.at[i])
        for i, (a, b) in enumerate(
            [(npos_hbm, npos), (cpos_hbm, cpos), (shot_hbm, shot), (qkv_hbm, qkv), (ck_hbm, ck), (cv_hbm, cv), (w_hbm, w)]
        )
    ]
    for load in loads:
        load.start()

    lane = lax.broadcasted_iota(jnp.int32, (1, HEAD_DIM), 1)
    even = lax.rem(lane, 2) == 0
    freq = frequencies()
    for load in loads[:3]:
        load.wait()
    first = lax.broadcasted_iota(jnp.int32, (3, 1), 0) == 0

    def angles_of(pos):
        return lax.dot_general(
            pos.astype(jnp.float32),
            freq,
            (((0,), (0,)), ((), ())),
            precision=lax.Precision.HIGHEST,
            preferred_element_type=jnp.float32,
        )

    angles[0 : RING * NEW_ROWS, :] = angles_of(npos[...] + jnp.where(first, SHOTS * SHOT_FRAMES, 0))
    angle = angles[pl.ds(pl.multiple_of(y * NEW_ROWS, NEW_ROWS), NEW_ROWS), :]
    cos = jnp.cos(angle)
    sin = jnp.where(even, -jnp.sin(angle), jnp.sin(angle))

    for load in loads[3:6]:
        load.wait()

    def rotate_new(i, carry):
        for j in range(HEADS_CORE):
            head = i * HEADS_CORE + j
            lanes = pl.ds(pl.multiple_of(head * HEAD_DIM, HEAD_DIM), HEAD_DIM)
            stage[head, 0] = turned(qkv[0, :, lanes], cos, sin, even)
            stage[head, 1] = turned(qkv[1, :, lanes], cos, sin, even)
            stage[head, 2] = qkv[2, :, lanes]
        return carry

    lax.fori_loop(0, D // (HEAD_DIM * HEADS_CORE), rotate_new, 0)
    angle = angles_of(cpos[...] + jnp.where(first, shot[...] * SHOT_FRAMES, 0))
    cos = jnp.cos(angle)
    sin = jnp.where(even, -jnp.sin(angle), jnp.sin(angle))
    for head in range(GROUP // HEAD_DIM):
        lanes = slice(head * HEAD_DIM, (head + 1) * HEAD_DIM)
        cstage[head, 0] = turned(ck[:, lanes], cos, sin, even)
        cstage[head, 1] = cv[:, lanes]
    @pl.when(core == 1)
    def _():
        pl.semaphore_wait(barrier, 2 * CORES * (RING - 1) + 1)
        pl.semaphore_signal(heard, inc=1, device_id=device(0, 0, 0, 1), device_id_type=MESH)

    @pl.when(core == 0)
    def _():
        pl.semaphore_wait(heard, 1)

    here = pl.multiple_of(core * OWN + y * NEW_ROWS, NEW_ROWS)
    q_rows = pl.ds(pl.multiple_of(z * CHIP_NEW + here, NEW_ROWS), NEW_ROWS)
    kv_rows = pl.ds(pl.multiple_of(ALL_CACHE + x * CHIP_NEW + here, NEW_ROWS), NEW_ROWS)
    sent = []

    def scatter(sems, offsets, parts):
        copies = []
        for d, dc in partners():
            k = d * CORES + dc
            src, dst, to = parts(d, dc)
            copy = pltpu.make_async_remote_copy(
                src, dst, sems[0].at[offsets, k], sems[1].at[offsets, k], device_id=to, device_id_type=MESH
            )
            sent.append(copy)
            copy.start()
            copies.append(copy)
        src, dst, _ = parts(0, 0)
        copy = pltpu.make_async_copy(src, dst, sems[1].at[offsets, 0])
        copy.start()
        copies.append(copy)
        return copies

    def arrive(copies):
        for copy in copies[:-1]:
            copy.wait_recv()
        copies[-1].wait()

    def new_part(first, heads, of_q):
        def parts(d, dc):
            to = (lax.rem(y + d, RING) * CORES + lax.rem(core + dc, CORES)) * HEADS_CORE
            src = stage.at[pl.ds(to + first, heads)]
            own = pl.ds(first, heads)
            if of_q:
                return src.at[:, 0], q.at[own, q_rows], device(0, d, 0, dc)
            return src.at[:, pl.ds(1, 2)], kv.at[own, :, kv_rows], device(0, d, 0, dc)

        return parts

    def cache_part(d, dc):
        src = cstage.at[pl.ds(lax.rem(core + dc, CORES) * HEADS_CORE, HEADS_CORE)]
        return src, kv.at[:, :, c_rows], device(d, 0, 0, dc)

    c_rows = pl.ds(pl.multiple_of(x * CHIP_CACHE + core * CACHE_ROWS, CACHE_ROWS), CACHE_ROWS)
    chip_kv = pl.ds(pl.multiple_of(ALL_CACHE + x * CHIP_NEW, CHIP_NEW), CHIP_NEW)
    chip_q = pl.ds(pl.multiple_of(z * CHIP_NEW, CHIP_NEW), CHIP_NEW)

    def along_x(head):
        copies = [
            pltpu.make_async_remote_copy(
                kv.at[head, :, chip_kv],
                kv.at[head, :, chip_kv],
                x_send.at[head, d],
                x_recv.at[head, d],
                device_id=device(d, 0, 0, 0),
                device_id_type=MESH,
            )
            for d in (2, 1, 3)
        ]
        for copy in copies:
            copy.start()
        sent.extend(copies)
        return copies

    def along_z(head):
        copies = [
            pltpu.make_async_remote_copy(
                q.at[head, chip_q],
                q.at[head, chip_q],
                z_send.at[head, d],
                z_recv.at[head, d],
                device_id=device(0, 0, d, 0),
                device_id_type=MESH,
            )
            for d in (2, 1, 3)
        ]
        for copy in copies:
            copy.start()
        sent.extend(copies)
        return copies

    def flush(copies):
        for copy in copies:
            copy.wait_send()
            sent[:] = [s for s in sent if s is not copy]

    a_sems = (a_send, a_recv)
    kv_in = [scatter(a_sems, 1, new_part(0, 1, False))]
    q_in = scatter(a_sems, 0, new_part(1, 2, True))
    cached = scatter((c_send, c_recv), 0, cache_part)
    kv_in.append(scatter(a_sems, 2, new_part(1, 2, False)))
    @pl.when(core == 0)
    def _():
        pl.semaphore_wait(barrier, CORES * (RING - 1) + 1)
        pl.semaphore_signal(heard, inc=1, device_id=device(0, 0, 0, 1), device_id_type=MESH)

    @pl.when(core == 1)
    def _():
        pl.semaphore_wait(heard, 1)

    for d in (2, 1, 3):
        pl.semaphore_signal(told, inc=1, device_id=device(0, d, 0, 0), device_id_type=MESH)
    pl.semaphore_wait(told, 3)
    straight = []
    for dx, dy, dz, at_core in crossed:
        dc = lax.rem(core + at_core, CORES) if dy or dz else 1
        to = (lax.rem(y + dy, RING) * CORES + lax.rem(core + dc, CORES)) * HEADS_CORE
        copy = pltpu.make_async_remote_copy(
            stage.at[to, 0],
            q.at[0, q_rows],
            f_send.at[0],
            f_recv.at[0],
            device_id=device(dx, dy, dz, dc),
            device_id_type=MESH,
        )
        copy.start()
    own_q = pltpu.make_async_copy(stage.at[(y * CORES + core) * HEADS_CORE, 0], q.at[0, q_rows], f_recv.at[1])
    own_q.start()

    arrive(kv_in[0])
    gathered_x = [along_x(0)]
    arrive(q_in)
    gathered_z = [[], along_z(1)]
    gathered_z.append(along_z(2))
    arrive(kv_in[1])
    gathered_x.append(along_x(1))
    gathered_x.append(along_x(2))
    arrive(cached)
    whole = q.at[0, pl.ds(0, QUERIES - NEW_ROWS)]
    pltpu.make_async_copy(whole, whole, f_recv.at[0]).wait()
    own_q.wait()

    def o_copy(head, d, dc):
        to_z = lax.rem(z + d, RING)
        to_core = lax.rem(core + dc, CORES)
        rows = pl.ds(pl.multiple_of(to_z * CHIP_NEW + to_core * OWN, OWN), OWN)
        k = d * CORES + dc
        return pltpu.make_async_remote_copy(
            o.at[head, rows],
            ored.at[z, core, head],
            o_send.at[head, k],
            o_recv.at[head, k],
            device_id=device(0, 0, d, dc),
            device_id_type=MESH,
        )

    for head in range(HEADS_CORE):
        for copy in gathered_x[head] + gathered_z[head]:
            copy.wait_recv()
        scores = lax.dot_general(q[head], kv[head, 0], (((1,), (1,)), ((), ())), preferred_element_type=jnp.float32)
        peak = jnp.max(scores, axis=1, keepdims=True)
        p = jnp.exp2((scores - peak) * SCALE2)
        total = jnp.sum(p, axis=1, keepdims=True)
        level = peak * SCALE2 + jnp.log2(total)
        lse[...] = jnp.where(lane == head, level, lse[...] if head else 0.0)
        if head == HEADS_CORE - 1:
            stats = []
            for s in range(RING):
                lse_t[s] = jnp.transpose(lse[s * CHIP_NEW : (s + 1) * CHIP_NEW, :])[0:8, :]
            for d, dc in partners():
                k = d * CORES + dc
                copy = pltpu.make_async_remote_copy(
                    lse_t.at[lax.rem(z + d, RING)],
                    lred.at[z, core],
                    l_send.at[k],
                    l_recv.at[k],
                    device_id=device(0, 0, d, dc),
                    device_id_type=MESH,
                )
                copy.start()
                stats.append(copy)
            lred[z, core] = lse_t[z]
            sent += stats
        mixed = jnp.dot(p.astype(jnp.bfloat16), kv[head, 1], preferred_element_type=jnp.float32)
        o[head] = (mixed / total).astype(jnp.bfloat16)
        for d, dc in partners():
            o_copy(head, d, dc).start()
        own = pl.ds(pl.multiple_of(z * CHIP_NEW + core * OWN, OWN), OWN)
        ored[z, core, head] = o[head, own]

    for copy in stats:
        copy.wait_recv()
    levels = lred[...]
    share = jnp.exp2(levels - jnp.max(levels, axis=0, keepdims=True))
    share = share / jnp.sum(share, axis=0, keepdims=True)
    columns = jnp.transpose(share.reshape(RING * CORES * 8, CHIP_NEW))
    weights[:, 0 : RING * CORES * 8] = columns
    mine_w = weights[pl.ds(pl.multiple_of(core * OWN, OWN), OWN), :]
    returned = [o_copy(head, d, dc) for head in range(HEADS_CORE) for d, dc in partners()]
    for copy in returned:
        copy.wait_recv()
    sent += returned
    attended = []
    for c in range(CORES):
        for head in range(HEADS_CORE):
            total = None
            for s in range(RING):
                at = (s * CORES + c) * 8 + head
                term = ored[s, c, head].astype(jnp.float32) * mine_w[:, at : at + 1]
                total = term if total is None else total + term
            attended.append(total.astype(jnp.bfloat16))
    attended = jnp.concatenate(attended, axis=1)

    loads[6].wait()
    summed = []
    for j in range(CHUNKS):
        cols = slice(j * CHUNK, (j + 1) * CHUNK)
        part[:, cols] = jnp.dot(attended, w[:, cols], preferred_element_type=jnp.float32).astype(jnp.bfloat16)
        of_chunk = []
        for d in (2, 1, 3):
            rows = pl.ds(pl.multiple_of(lax.rem(y + d, RING) * NEW_ROWS, NEW_ROWS), NEW_ROWS)
            copy = pltpu.make_async_remote_copy(
                part.at[rows, pl.ds(j * CHUNK, CHUNK)],
                recv.at[d, :, pl.ds(j * CHUNK, CHUNK)],
                y_send.at[j, d],
                y_recv.at[j, d],
                device_id=device(0, d, 0, 0),
                device_id_type=MESH,
            )
            copy.start()
            of_chunk.append(copy)
        summed.append(of_chunk)
        sent += of_chunk
    rows = pl.ds(pl.multiple_of(y * NEW_ROWS, NEW_ROWS), NEW_ROWS)
    for j in range(CHUNKS):
        cols = slice(j * CHUNK, (j + 1) * CHUNK)
        for copy in summed[j]:
            copy.wait_recv()
        total = part[rows, cols].astype(jnp.float32)
        for d in (1, 2, 3):
            total = total + recv[d, :, cols].astype(jnp.float32)
        out_ref[:, cols] = total.astype(jnp.bfloat16)

    for copy in sent:
        copy.wait_send()
    pltpu.make_async_copy(whole, whole, f_send.at[0]).wait()


def on_device(new_qkv, new_pos, cache_keys, cache_values, cache_pos, cache_shot, out_weight):
    bf16, f32, i32 = jnp.bfloat16, jnp.float32, jnp.int32
    dma = pltpu.SemaphoreType.DMA
    partners = RING * CORES
    return pl.pallas_call(
        kernel,
        out_shape=jax.ShapeDtypeStruct((NEW_ROWS, D), bf16),
        in_specs=[pl.BlockSpec(memory_space=pl.ANY)] * 7,
        out_specs=pl.BlockSpec(memory_space=pltpu.VMEM),
        scratch_shapes=[
            pltpu.VMEM((3, NEW_ROWS, D), bf16),
            pltpu.VMEM((3, RING * NEW_ROWS), i32),
            pltpu.VMEM((CACHE_ROWS, GROUP), bf16),
            pltpu.VMEM((CACHE_ROWS, GROUP), bf16),
            pltpu.VMEM((3, CACHE_ROWS), i32),
            pltpu.VMEM((1, CACHE_ROWS), i32),
            pltpu.VMEM((GROUP, D), bf16),
            pltpu.VMEM((RING * NEW_ROWS, HEAD_DIM), f32),
            pltpu.VMEM((D // HEAD_DIM, 3, NEW_ROWS, HEAD_DIM), bf16),
            pltpu.VMEM((GROUP // HEAD_DIM, 2, CACHE_ROWS, HEAD_DIM), bf16),
            pltpu.VMEM((HEADS_CORE, 2, KEYS, HEAD_DIM), bf16),
            pltpu.VMEM((HEADS_CORE, QUERIES, HEAD_DIM), bf16),
            pltpu.VMEM((HEADS_CORE, QUERIES, HEAD_DIM), bf16),
            pltpu.VMEM((QUERIES, HEAD_DIM), f32),
            pltpu.VMEM((RING, 8, CHIP_NEW), f32),
            pltpu.VMEM((RING, CORES, HEADS_CORE, OWN, HEAD_DIM), bf16),
            pltpu.VMEM((RING, CORES, 8, CHIP_NEW), f32),
            pltpu.VMEM((CHIP_NEW, HEAD_DIM), f32),
            pltpu.VMEM((OWN, D), bf16),
            pltpu.VMEM((RING, NEW_ROWS, D), bf16),
            dma((7,)),
            pltpu.SemaphoreType.REGULAR,
            pltpu.SemaphoreType.REGULAR,
            dma((1,)),
            dma((2,)),
            dma((4, partners)),
            dma((4, partners)),
            dma((1, partners)),
            dma((1, partners)),
            dma((HEADS_CORE, RING)),
            dma((HEADS_CORE, RING)),
            dma((HEADS_CORE, RING)),
            dma((HEADS_CORE, RING)),
            dma((HEADS_CORE, partners)),
            dma((HEADS_CORE, partners)),
            dma((partners,)),
            dma((partners,)),
            dma((CHUNKS, RING)),
            dma((CHUNKS, RING)),
        ],
        compiler_params=pltpu.CompilerParams(collective_id=0, has_side_effects=True, vmem_limit_bytes=32 << 20),
        name="shot_attention",
    )(
        *(
            pltpu.with_memory_space_constraint(a, pltpu.HBM)
            for a in (
                jnp.transpose(new_qkv, (1, 0, 2)),
                new_pos,
                cache_keys,
                cache_values,
                cache_pos,
                cache_shot.reshape(1, CACHE_ROWS),
                out_weight,
            )
        )
    )


def solution(mesh):
    placed = (
        P(("batch", "frame", "head"), None, None),
        P("batch", "frame"),
        P(("batch", "frame"), "head"),
        P(("batch", "frame"), "head"),
        P("batch", "frame"),
        P(("batch", "frame")),
        P("head", None),
    )
    return jax.shard_map(
        on_device,
        mesh=mesh,
        in_specs=placed,
        out_specs=P(("batch", "frame", "head"), None),
        check_vma=False,
    )
```

```python
import functools
import math

import jax
import jax.numpy as jnp
from jax import lax
from jax.experimental import pallas as pl
from jax.experimental.pallas import tpu as pltpu
from jax.sharding import PartitionSpec as P

HEAD_DIM = 128
SHOTS = 3
SHOT_FRAMES = 8
THETA = 10000.0
RING = 4
CORES = 2
NEW_ROWS = 16
CACHE_ROWS = 32
HEADS_CORE = 3
CHIP_NEW = RING * CORES * NEW_ROWS
CHIP_CACHE = CORES * CACHE_ROWS
ALL_CACHE = RING * CHIP_CACHE
KEYS = RING * (CHIP_NEW + CHIP_CACHE)
QUERIES = RING * CHIP_NEW
OWN = RING * NEW_ROWS
D = 3072
GROUP = D // RING
CHUNKS = 3
CHUNK = D // CHUNKS
SCALE2 = math.log2(math.e) / math.sqrt(HEAD_DIM)
MESH = pl.DeviceIdType.MESH


def frequencies():
    lanes = lax.broadcasted_iota(jnp.int32, (3, HEAD_DIM), 1)
    part = lax.broadcasted_iota(jnp.int32, (3, HEAD_DIM), 0)
    pairs = lanes // 2
    time_pairs = HEAD_DIM // 16
    row_pairs = (HEAD_DIM // 2 - time_pairs) // 2
    rest_pairs = HEAD_DIM // 2 - time_pairs - row_pairs
    of_part = jnp.where(pairs < time_pairs, 0, jnp.where(pairs < time_pairs + row_pairs, 1, 2))
    pair_float = pairs.astype(jnp.float32)
    exponent = jnp.where(
        of_part == 0,
        pair_float / time_pairs,
        jnp.where(
            of_part == 1,
            (pair_float - time_pairs) / row_pairs,
            (pair_float - time_pairs - row_pairs) / rest_pairs,
        ),
    )
    return jnp.where(of_part == part, jnp.exp(exponent * -math.log(THETA)), 0.0)


def turned(block, cos, sin, even):
    x = block.astype(jnp.float32)
    partner = jnp.where(even, pltpu.roll(x, HEAD_DIM - 1, 1), pltpu.roll(x, 1, 1))
    return (x * cos + partner * sin).astype(jnp.bfloat16)


def kernel(
    qkv_hbm,
    npos_hbm,
    ck_hbm,
    cv_hbm,
    cpos_hbm,
    shot_hbm,
    w_hbm,
    out_ref,
    qkv,
    npos,
    ck,
    cv,
    cpos,
    shot,
    w,
    angles,
    stage,
    cstage,
    kv,
    q,
    o,
    lse,
    lse_t,
    ored,
    lred,
    weights,
    part,
    recv,
    in_sem,
    heard,
    told,
    f_send,
    f_recv,
    a_send,
    a_recv,
    c_send,
    c_recv,
    x_send,
    x_recv,
    z_send,
    z_recv,
    o_send,
    o_recv,
    l_send,
    l_recv,
    y_send,
    y_recv,
):
    frame = lax.axis_index("frame")
    y = lax.axis_index("head")
    batch = lax.axis_index("batch")
    core = lax.rem(frame, CORES)
    x = lax.rem(frame // CORES, RING)
    z = frame // (CORES * RING)

    def device(dx, dy, dz, dc):
        to = (lax.rem(z + dz, RING) * RING + lax.rem(x + dx, RING)) * CORES + lax.rem(core + dc, CORES)
        return (to, lax.rem(y + dy, RING), batch)

    def partners():
        for to_core in (0, 1):
            for d in (2, 1, 3):
                yield d, lax.rem(core + to_core, CORES)
        yield 0, 1

    barrier = pltpu.get_barrier_semaphore()
    for d in (2, 1, 3):
        pl.semaphore_signal(barrier, inc=1, device_id=device(0, 0, d, core), device_id_type=MESH)
    for d in (2, 1, 3):
        pl.semaphore_signal(barrier, inc=1, device_id=device(0, d, 0, 1 - core), device_id_type=MESH)
        pl.semaphore_signal(barrier, inc=1, device_id=device(d, 0, 0, 1 - core), device_id_type=MESH)
    pl.semaphore_signal(barrier, inc=1, device_id=device(0, 0, 0, 1), device_id_type=MESH)

    crossed = [(0, dy, dz, c) for dz in (2, 1, 3, 0) for c in (0, 1) for dy in (2, 1, 3, 0) if dy or dz or c]
    loads = [
        pltpu.make_async_copy(a, b, in_sem.at[i])
        for i, (a, b) in enumerate(
            [(npos_hbm, npos), (cpos_hbm, cpos), (shot_hbm, shot), (qkv_hbm, qkv), (ck_hbm, ck), (cv_hbm, cv), (w_hbm, w)]
        )
    ]
    for load in loads:
        load.start()

    lane = lax.broadcasted_iota(jnp.int32, (1, HEAD_DIM), 1)
    even = lax.rem(lane, 2) == 0
    freq = frequencies()
    for load in loads[:3]:
        load.wait()
    first = lax.broadcasted_iota(jnp.int32, (3, 1), 0) == 0

    def angles_of(pos):
        return lax.dot_general(
            pos.astype(jnp.float32),
            freq,
            (((0,), (0,)), ((), ())),
            precision=lax.Precision.HIGHEST,
            preferred_element_type=jnp.float32,
        )

    angles[0 : RING * NEW_ROWS, :] = angles_of(npos[...] + jnp.where(first, SHOTS * SHOT_FRAMES, 0))
    angle = angles[pl.ds(pl.multiple_of(y * NEW_ROWS, NEW_ROWS), NEW_ROWS), :]
    cos = jnp.cos(angle)
    sin = jnp.where(even, -jnp.sin(angle), jnp.sin(angle))

    for load in loads[3:6]:
        load.wait()

    def rotate_new(i, carry):
        for j in range(HEADS_CORE):
            head = i * HEADS_CORE + j
            lanes = pl.ds(pl.multiple_of(head * HEAD_DIM, HEAD_DIM), HEAD_DIM)
            stage[head, 0] = turned(qkv[0, :, lanes], cos, sin, even)
            stage[head, 1] = turned(qkv[1, :, lanes], cos, sin, even)
            stage[head, 2] = qkv[2, :, lanes]
        return carry

    lax.fori_loop(0, D // (HEAD_DIM * HEADS_CORE), rotate_new, 0)
    angle = angles_of(cpos[...] + jnp.where(first, shot[...] * SHOT_FRAMES, 0))
    cos = jnp.cos(angle)
    sin = jnp.where(even, -jnp.sin(angle), jnp.sin(angle))
    for head in range(GROUP // HEAD_DIM):
        lanes = slice(head * HEAD_DIM, (head + 1) * HEAD_DIM)
        cstage[head, 0] = turned(ck[:, lanes], cos, sin, even)
        cstage[head, 1] = cv[:, lanes]
    @pl.when(core == 1)
    def _():
        pl.semaphore_wait(barrier, 2 * CORES * (RING - 1) + 1)
        pl.semaphore_signal(heard, inc=1, device_id=device(0, 0, 0, 1), device_id_type=MESH)

    @pl.when(core == 0)
    def _():
        pl.semaphore_wait(heard, 1)

    here = pl.multiple_of(core * OWN + y * NEW_ROWS, NEW_ROWS)
    q_rows = pl.ds(pl.multiple_of(z * CHIP_NEW + here, NEW_ROWS), NEW_ROWS)
    kv_rows = pl.ds(pl.multiple_of(ALL_CACHE + x * CHIP_NEW + here, NEW_ROWS), NEW_ROWS)
    sent = []

    def scatter(sems, offsets, parts):
        copies = []
        for d, dc in partners():
            k = d * CORES + dc
            src, dst, to = parts(d, dc)
            copy = pltpu.make_async_remote_copy(
                src, dst, sems[0].at[offsets, k], sems[1].at[offsets, k], device_id=to, device_id_type=MESH
            )
            sent.append(copy)
            copy.start()
            copies.append(copy)
        src, dst, _ = parts(0, 0)
        copy = pltpu.make_async_copy(src, dst, sems[1].at[offsets, 0])
        copy.start()
        copies.append(copy)
        return copies

    def arrive(copies):
        for copy in copies[:-1]:
            copy.wait_recv()
        copies[-1].wait()

    def new_part(first, heads, of_q):
        def parts(d, dc):
            to = (lax.rem(y + d, RING) * CORES + lax.rem(core + dc, CORES)) * HEADS_CORE
            src = stage.at[pl.ds(to + first, heads)]
            own = pl.ds(first, heads)
            if of_q:
                return src.at[:, 0], q.at[own, q_rows], device(0, d, 0, dc)
            return src.at[:, pl.ds(1, 2)], kv.at[own, :, kv_rows], device(0, d, 0, dc)

        return parts

    def cache_part(d, dc):
        src = cstage.at[pl.ds(lax.rem(core + dc, CORES) * HEADS_CORE, HEADS_CORE)]
        return src, kv.at[:, :, c_rows], device(d, 0, 0, dc)

    c_rows = pl.ds(pl.multiple_of(x * CHIP_CACHE + core * CACHE_ROWS, CACHE_ROWS), CACHE_ROWS)
    chip_kv = pl.ds(pl.multiple_of(ALL_CACHE + x * CHIP_NEW, CHIP_NEW), CHIP_NEW)
    chip_q = pl.ds(pl.multiple_of(z * CHIP_NEW, CHIP_NEW), CHIP_NEW)

    def along_x(head):
        copies = [
            pltpu.make_async_remote_copy(
                kv.at[head, :, chip_kv],
                kv.at[head, :, chip_kv],
                x_send.at[head, d],
                x_recv.at[head, d],
                device_id=device(d, 0, 0, 0),
                device_id_type=MESH,
            )
            for d in (2, 1, 3)
        ]
        for copy in copies:
            copy.start()
        sent.extend(copies)
        return copies

    def along_z(head):
        copies = [
            pltpu.make_async_remote_copy(
                q.at[head, chip_q],
                q.at[head, chip_q],
                z_send.at[head, d],
                z_recv.at[head, d],
                device_id=device(0, 0, d, 0),
                device_id_type=MESH,
            )
            for d in (2, 1, 3)
        ]
        for copy in copies:
            copy.start()
        sent.extend(copies)
        return copies

    def flush(copies):
        for copy in copies:
            copy.wait_send()
            sent[:] = [s for s in sent if s is not copy]

    a_sems = (a_send, a_recv)
    kv_in = [scatter(a_sems, 1, new_part(0, 1, False))]
    q_in = scatter(a_sems, 0, new_part(1, 2, True))
    cached = scatter((c_send, c_recv), 0, cache_part)
    kv_in.append(scatter(a_sems, 2, new_part(1, 2, False)))
    @pl.when(core == 0)
    def _():
        pl.semaphore_wait(barrier, CORES * (RING - 1) + 1)
        pl.semaphore_signal(heard, inc=1, device_id=device(0, 0, 0, 1), device_id_type=MESH)

    @pl.when(core == 1)
    def _():
        pl.semaphore_wait(heard, 1)

    for d in (2, 1, 3):
        pl.semaphore_signal(told, inc=1, device_id=device(0, d, 0, 0), device_id_type=MESH)
    pl.semaphore_wait(told, 3)
    straight = []
    for dx, dy, dz, at_core in crossed:
        dc = lax.rem(core + at_core, CORES) if dy or dz else 1
        to = (lax.rem(y + dy, RING) * CORES + lax.rem(core + dc, CORES)) * HEADS_CORE
        copy = pltpu.make_async_remote_copy(
            stage.at[to, 0],
            q.at[0, q_rows],
            f_send.at[0],
            f_recv.at[0],
            device_id=device(dx, dy, dz, dc),
            device_id_type=MESH,
        )
        copy.start()
    own_q = pltpu.make_async_copy(stage.at[(y * CORES + core) * HEADS_CORE, 0], q.at[0, q_rows], f_recv.at[1])
    own_q.start()

    arrive(kv_in[0])
    gathered_x = [along_x(0)]
    arrive(q_in)
    gathered_z = [[], along_z(1)]
    gathered_z.append(along_z(2))
    arrive(kv_in[1])
    gathered_x.append(along_x(1))
    gathered_x.append(along_x(2))
    arrive(cached)
    whole = q.at[0, pl.ds(0, QUERIES - NEW_ROWS)]
    pltpu.make_async_copy(whole, whole, f_recv.at[0]).wait()
    own_q.wait()

    def o_copy(head, d, dc):
        to_z = lax.rem(z + d, RING)
        to_core = lax.rem(core + dc, CORES)
        rows = pl.ds(pl.multiple_of(to_z * CHIP_NEW + to_core * OWN, OWN), OWN)
        k = d * CORES + dc
        return pltpu.make_async_remote_copy(
            o.at[head, rows],
            ored.at[z, core, head],
            o_send.at[head, k],
            o_recv.at[head, k],
            device_id=device(0, 0, d, dc),
            device_id_type=MESH,
        )

    for head in range(HEADS_CORE):
        for copy in gathered_x[head] + gathered_z[head]:
            copy.wait_recv()
        scores = lax.dot_general(q[head], kv[head, 0], (((1,), (1,)), ((), ())), preferred_element_type=jnp.float32)
        peak = jnp.max(scores, axis=1, keepdims=True)
        p = jnp.exp2((scores - peak) * SCALE2)
        total = jnp.sum(p, axis=1, keepdims=True)
        level = peak * SCALE2 + jnp.log2(total)
        lse[...] = jnp.where(lane == head, level, lse[...] if head else 0.0)
        if head == HEADS_CORE - 1:
            stats = []
            for s in range(RING):
                lse_t[s] = jnp.transpose(lse[s * CHIP_NEW : (s + 1) * CHIP_NEW, :])[0:8, :]
            for d, dc in partners():
                k = d * CORES + dc
                copy = pltpu.make_async_remote_copy(
                    lse_t.at[lax.rem(z + d, RING)],
                    lred.at[z, core],
                    l_send.at[k],
                    l_recv.at[k],
                    device_id=device(0, 0, d, dc),
                    device_id_type=MESH,
                )
                copy.start()
                stats.append(copy)
            lred[z, core] = lse_t[z]
            sent += stats
        mixed = jnp.dot(p.astype(jnp.bfloat16), kv[head, 1], preferred_element_type=jnp.float32)
        o[head] = (mixed / total).astype(jnp.bfloat16)
        for d, dc in partners():
            o_copy(head, d, dc).start()
        own = pl.ds(pl.multiple_of(z * CHIP_NEW + core * OWN, OWN), OWN)
        ored[z, core, head] = o[head, own]

    for copy in stats:
        copy.wait_recv()
    levels = lred[...]
    share = jnp.exp2(levels - jnp.max(levels, axis=0, keepdims=True))
    share = share / jnp.sum(share, axis=0, keepdims=True)
    columns = jnp.transpose(share.reshape(RING * CORES * 8, CHIP_NEW))
    weights[:, 0 : RING * CORES * 8] = columns
    mine_w = weights[pl.ds(pl.multiple_of(core * OWN, OWN), OWN), :]
    attended = [None] * (CORES * HEADS_CORE)
    for head in range(HEADS_CORE):
        returned = [o_copy(head, d, dc) for d, dc in partners()]
        for copy in returned:
            copy.wait_recv()
        sent += returned
        for c in range(CORES):
            total = None
            for s in range(RING):
                at = (s * CORES + c) * 8 + head
                term = ored[s, c, head].astype(jnp.float32) * mine_w[:, at : at + 1]
                total = term if total is None else total + term
            attended[c * HEADS_CORE + head] = total.astype(jnp.bfloat16)
    attended = jnp.concatenate(attended, axis=1)

    loads[6].wait()
    summed = []
    for j in range(CHUNKS):
        cols = slice(j * CHUNK, (j + 1) * CHUNK)
        part[:, cols] = jnp.dot(attended, w[:, cols], preferred_element_type=jnp.float32).astype(jnp.bfloat16)
        of_chunk = []
        for d in (2, 1, 3):
            rows = pl.ds(pl.multiple_of(lax.rem(y + d, RING) * NEW_ROWS, NEW_ROWS), NEW_ROWS)
            copy = pltpu.make_async_remote_copy(
                part.at[rows, pl.ds(j * CHUNK, CHUNK)],
                recv.at[d, :, pl.ds(j * CHUNK, CHUNK)],
                y_send.at[j, d],
                y_recv.at[j, d],
                device_id=device(0, d, 0, 0),
                device_id_type=MESH,
            )
            copy.start()
            of_chunk.append(copy)
        summed.append(of_chunk)
        sent += of_chunk
    rows = pl.ds(pl.multiple_of(y * NEW_ROWS, NEW_ROWS), NEW_ROWS)
    for j in range(CHUNKS):
        cols = slice(j * CHUNK, (j + 1) * CHUNK)
        for copy in summed[j]:
            copy.wait_recv()
        total = part[rows, cols].astype(jnp.float32)
        for d in (1, 2, 3):
            total = total + recv[d, :, cols].astype(jnp.float32)
        out_ref[:, cols] = total.astype(jnp.bfloat16)

    for copy in sent:
        copy.wait_send()
    pltpu.make_async_copy(whole, whole, f_send.at[0]).wait()


def on_device(new_qkv, new_pos, cache_keys, cache_values, cache_pos, cache_shot, out_weight):
    bf16, f32, i32 = jnp.bfloat16, jnp.float32, jnp.int32
    dma = pltpu.SemaphoreType.DMA
    partners = RING * CORES
    return pl.pallas_call(
        kernel,
        out_shape=jax.ShapeDtypeStruct((NEW_ROWS, D), bf16),
        in_specs=[pl.BlockSpec(memory_space=pl.ANY)] * 7,
        out_specs=pl.BlockSpec(memory_space=pltpu.VMEM),
        scratch_shapes=[
            pltpu.VMEM((3, NEW_ROWS, D), bf16),
            pltpu.VMEM((3, RING * NEW_ROWS), i32),
            pltpu.VMEM((CACHE_ROWS, GROUP), bf16),
            pltpu.VMEM((CACHE_ROWS, GROUP), bf16),
            pltpu.VMEM((3, CACHE_ROWS), i32),
            pltpu.VMEM((1, CACHE_ROWS), i32),
            pltpu.VMEM((GROUP, D), bf16),
            pltpu.VMEM((RING * NEW_ROWS, HEAD_DIM), f32),
            pltpu.VMEM((D // HEAD_DIM, 3, NEW_ROWS, HEAD_DIM), bf16),
            pltpu.VMEM((GROUP // HEAD_DIM, 2, CACHE_ROWS, HEAD_DIM), bf16),
            pltpu.VMEM((HEADS_CORE, 2, KEYS, HEAD_DIM), bf16),
            pltpu.VMEM((HEADS_CORE, QUERIES, HEAD_DIM), bf16),
            pltpu.VMEM((HEADS_CORE, QUERIES, HEAD_DIM), bf16),
            pltpu.VMEM((QUERIES, HEAD_DIM), f32),
            pltpu.VMEM((RING, 8, CHIP_NEW), f32),
            pltpu.VMEM((RING, CORES, HEADS_CORE, OWN, HEAD_DIM), bf16),
            pltpu.VMEM((RING, CORES, 8, CHIP_NEW), f32),
            pltpu.VMEM((CHIP_NEW, HEAD_DIM), f32),
            pltpu.VMEM((OWN, D), bf16),
            pltpu.VMEM((RING, NEW_ROWS, D), bf16),
            dma((7,)),
            pltpu.SemaphoreType.REGULAR,
            pltpu.SemaphoreType.REGULAR,
            dma((1,)),
            dma((2,)),
            dma((4, partners)),
            dma((4, partners)),
            dma((1, partners)),
            dma((1, partners)),
            dma((HEADS_CORE, RING)),
            dma((HEADS_CORE, RING)),
            dma((HEADS_CORE, RING)),
            dma((HEADS_CORE, RING)),
            dma((HEADS_CORE, partners)),
            dma((HEADS_CORE, partners)),
            dma((partners,)),
            dma((partners,)),
            dma((CHUNKS, RING)),
            dma((CHUNKS, RING)),
        ],
        compiler_params=pltpu.CompilerParams(collective_id=0, has_side_effects=True, vmem_limit_bytes=32 << 20),
        name="shot_attention",
    )(
        *(
            pltpu.with_memory_space_constraint(a, pltpu.HBM)
            for a in (
                jnp.transpose(new_qkv, (1, 0, 2)),
                new_pos,
                cache_keys,
                cache_values,
                cache_pos,
                cache_shot.reshape(1, CACHE_ROWS),
                out_weight,
            )
        )
    )


def solution(mesh):
    placed = (
        P(("batch", "frame", "head"), None, None),
        P("batch", "frame"),
        P(("batch", "frame"), "head"),
        P(("batch", "frame"), "head"),
        P("batch", "frame"),
        P(("batch", "frame")),
        P("head", None),
    )
    return jax.shard_map(
        on_device,
        mesh=mesh,
        in_specs=placed,
        out_specs=P(("batch", "frame", "head"), None),
        check_vma=False,
    )
```
